32 devices in a mesh: slides: 2 (over y), tile: 4 (over z), col: 2 (over x), mp: 2 (over core).
Axes of the slice: x: 2, y: 2, z: 4, core: 2. Of those that a mesh axis runs over, the one named last changes fastest.
Arguments:
- patches: bfloat16 [128, 48, 1024], P(('slides', 'tile'), 'col', 'mp'), parts along dimension 0, may hold values from -8 to 8
- tissue: int32 [128, 48], P(('slides', 'tile'), 'col'), parts along dimension 0, may hold values from 0 to 1, as said below
- conv_weight: bfloat16 [3, 3, 1024], P(None, None, 'mp'), may hold values from -2 to 2
- ln_gain: float32 [1024], P('mp'), may hold values from 0.1 to 1.9
- qkv_weight: bfloat16 [3, 1024, 1024], P(None, None, 'mp'), may hold values from -0.1875 to 0.1875
- omega: float32 [256, 64], replicated, may hold values from -6 to 6
- out_weight: bfloat16 [1024, 1024], P('mp'), may hold values from -0.1875 to 0.1875
Outputs:
- layer_out: bfloat16 [128, 48, 1024], P(('slides', 'tile'), 'col', 'mp'), parts along dimension 0
The draws below stay inside these ranges and needn't reach their ends.
There are 2 independent parts, one for each index of `slides`. The reference program is written for one: setup_inputs(seed, part) draws one part's arguments, and reference() takes and returns one part's arrays. A program takes and returns all parts, laid end to end along the dimension named above; an argument that names none is the same for every part. Nothing has to cross between parts.
Inputs may be any that keep to these rules, and one draw needn't show every extreme that they name: 1 marks tissue, 0 background; the slide's first patch is tissue.
All inputs are finite; a program needn't handle non-finite values.
Results may differ from the reference program's by a relative error of at most 0.0065.
Values may be sent and summed in bfloat16 or wider, within the bound.
A program may use at most 64 MiB of HBM per device.

```python
import math
import jax
import jax.numpy as jnp
from jax import lax

D = 1024
H = 16
E = 64
M = 256
RT = 16
CT = 24
HP = 64
WP = 48


def draw_patches(key, part):
    noise_key = jax.random.fold_in(key, 11)
    region_key = jax.random.fold_in(key, 12)
    noise = jax.random.normal(noise_key, (HP, WP, D), jnp.float32)
    region = jax.random.normal(region_key, (HP // RT, WP // CT, D), jnp.float32)
    region = jnp.repeat(jnp.repeat(region, RT, axis=0), CT, axis=1)
    return jnp.clip(noise + region, -8.0, 8.0).astype(jnp.bfloat16)


def draw_tissue(key, part):
    level_key = jax.random.fold_in(key, 21)
    value_key = jax.random.fold_in(key, 22)
    levels = jax.random.randint(level_key, (HP // RT, WP // CT), 5, 100)
    levels = jnp.repeat(jnp.repeat(levels, RT, axis=0), CT, axis=1)
    values = jax.random.randint(value_key, (HP, WP), 0, 100)
    marked = jnp.where(values < levels, 1, 0).astype(jnp.int32)
    return marked.at[0, 0].set(1)


def shard_levels(stream_key, shape, split, least, top_value):
    factor_of, own = 1.0, jax.random.fold_in(stream_key, 6)
    for dim, parts in split:
        heights = jnp.exp(jax.random.uniform(jax.random.fold_in(own, dim), (parts,), jnp.float32, least / len(split), top_value / len(split)))
        factor_of = factor_of * jnp.repeat(heights, shape[dim] // parts).reshape([-1 if axis == dim else 1 for axis in range(len(shape))])
    return factor_of


def centred(stream_key, shape, deviation, limit, cuts=(), kind=jnp.bfloat16):
    gain = shard_levels(stream_key, shape, cuts, -0.22, 0.18) if cuts else 1.0
    values = jax.random.normal(stream_key, shape, jnp.float32) * deviation * gain
    return jnp.minimum(jnp.maximum(values, -limit), limit).astype(kind)


def setup_inputs(seed: int = 0, part: int = 0) -> dict:
    streams_of = jax.random.split(jax.random.key(seed), 8)
    part_keys = jax.random.split(jax.random.fold_in(streams_of[7], part), 8)
    return {
        "patches": draw_patches(jax.random.fold_in(jax.random.fold_in(streams_of[7], part), 71), part),
        "tissue": draw_tissue(jax.random.fold_in(jax.random.fold_in(streams_of[7], part), 71), part),
        "conv_weight": centred(streams_of[2], (3, 3, D), 9 ** -0.5, 2.0, ((2, 2),)),
        "ln_gain": jnp.clip(1.0 + 0.18 * jax.random.normal(streams_of[3], (D,), jnp.float32), 0.1, 1.9),
        "qkv_weight": centred(streams_of[4], (3, D, D), D ** -0.5, 0.1875, ((2, 2),)),
        "omega": centred(streams_of[5], (M, E), 1.0, 6.0, (), jnp.float32),
        "out_weight": centred(streams_of[6], (D, D), D ** -0.5, 0.1875, ((0, 2),)),
    }


def features(scaled, omega):
    lifted = jnp.einsum('the,me->thm', scaled, omega, precision=lax.Precision.HIGHEST)
    square = 0.5 * lax.optimization_barrier(jnp.sum(scaled * scaled, axis=-1, keepdims=True))
    return (jnp.exp(lifted - square) / math.sqrt(M)).astype(jnp.bfloat16)

def reference(patches, tissue, conv_weight, ln_gain, qkv_weight, omega, out_weight):
    plain = patches.astype(jnp.float32)
    padded = jnp.pad(plain, ((1, 1), (1, 1), (0, 0)))
    kernel = conv_weight.astype(jnp.float32)
    stem = plain
    for row_off in range(3):
        for col_off in range(3):
            stem = stem + kernel[row_off, col_off] * padded[row_off:row_off + HP, col_off:col_off + WP]
    mean_val = lax.optimization_barrier(jnp.mean(stem, axis=-1, keepdims=True))
    var_val = lax.optimization_barrier(jnp.mean(stem * stem, axis=-1, keepdims=True)) - mean_val * mean_val
    normed = ((stem - mean_val) * lax.rsqrt(var_val + 1e-05) * ln_gain).astype(jnp.bfloat16)
    scale = E ** (-0.25)
    block_rows = normed.reshape(HP // RT, RT * WP, D)
    block_keep = tissue.reshape(HP // RT, RT * WP).astype(jnp.float32)
    block_stem = stem.reshape(HP // RT, RT * WP, D)

    def keys(carry, item):
        rows, keep = item
        pair = jnp.einsum('td,cdf->ctf', rows.astype(jnp.float32), qkv_weight[1:].astype(jnp.float32)).astype(jnp.bfloat16)
        key_part = pair[0].astype(jnp.float32).reshape(-1, H, E) * scale
        value_part = pair[1].astype(jnp.float32).reshape(-1, H, E)
        key_feat = features(key_part, omega).astype(jnp.float32) * keep[:, None, None]
        state = carry[0] + jnp.einsum('the,thm->hem', value_part, key_feat, precision=lax.Precision.HIGHEST)
        totals = carry[1] + lax.optimization_barrier(jnp.sum(key_feat, axis=0))
        return ((state, totals), None)
    start = (jnp.zeros((H, E, M), jnp.float32), jnp.zeros((H, M), jnp.float32))
    (kv_state, normalizer), unused = lax.scan(keys, start, (block_rows, block_keep))

    def queries(item):
        rows, stem_rows = item
        query = jnp.dot(rows, qkv_weight[0], preferred_element_type=jnp.float32).astype(jnp.bfloat16)
        query_part = query.astype(jnp.float32).reshape(-1, H, E) * scale
        query_feat = features(query_part, omega).astype(jnp.float32)
        numer = jnp.einsum('thm,hem->the', query_feat, kv_state, precision=lax.Precision.HIGHEST)
        denom = jnp.einsum('thm,hm->th', query_feat, normalizer, precision=lax.Precision.HIGHEST)
        attended = (numer / denom[:, :, None]).astype(jnp.bfloat16).reshape(-1, D)
        mixed = jnp.dot(attended, out_weight, preferred_element_type=jnp.float32)
        return (stem_rows + mixed).astype(jnp.bfloat16)
    result = lax.map(queries, (block_rows, block_stem))
    return result.reshape(HP, WP, D)
```

```python
import functools
import math

import jax
import jax.numpy as jnp
from jax import lax
from jax.experimental import pallas as pl
from jax.experimental.pallas import tpu as pltpu
from jax.sharding import PartitionSpec as P

E = 64
M = 256


def extended(cells, sides, width):
    for axis, dim in sides:
        count = lax.axis_size(axis)
        ends = count - 1
        head = lax.slice_in_dim(cells, 0, width, axis=dim)
        tail = lax.slice_in_dim(cells, cells.shape[dim] - width, cells.shape[dim], axis=dim)
        cells = jnp.concatenate(
            [
                lax.ppermute(tail, axis, [(i, (i + 1) % count) for i in range(ends)]),
                cells,
                lax.ppermute(head, axis, [((i + 1) % count, i) for i in range(ends)]),
            ],
            axis=dim,
        )
    return cells


def features(scaled, omega):
    lifted = jnp.einsum("the,me->thm", scaled, omega, precision=lax.Precision.HIGHEST)
    square = 0.5 * jnp.sum(scaled * scaled, axis=-1, keepdims=True)
    return (jnp.exp(lifted - square) / math.sqrt(M)).astype(jnp.bfloat16)


def split_pair(values):
    upper = values.astype(jnp.bfloat16)
    lower = (values - upper.astype(jnp.float32)).astype(jnp.bfloat16)
    return (upper, lower)


def shards(patches, tissue, conv_weight, ln_gain, qkv_weight, omega, out_weight):
    rows_here, cols_here, half = patches.shape
    tokens = rows_here * cols_here
    padded = extended(patches, (("tile", 0), ("col", 1)), 1)
    widened = padded.astype(jnp.float32)
    kernel = conv_weight.astype(jnp.float32)
    stem = patches.astype(jnp.float32)
    for row_off in range(3):
        for col_off in range(3):
            stem = (
                stem
                + kernel[row_off, col_off]
                * widened[row_off : row_off + rows_here, col_off : col_off + cols_here]
            )
    flat = stem.reshape(tokens, half)
    totals = lax.psum((jnp.sum(flat, axis=1), jnp.sum(flat * flat, axis=1)), "mp")
    width = half * lax.axis_size("mp")
    mean_val = totals[0] / width
    var_val = totals[1] / width - mean_val * mean_val
    normed = ((flat - mean_val[:, None]) * lax.rsqrt(var_val + 1e-05)[:, None] * ln_gain).astype(
        jnp.bfloat16
    )
    projected = jnp.einsum(
        "td,cdf->ctf",
        lax.all_gather(normed, "mp", axis=1, tiled=True),
        qkv_weight,
        preferred_element_type=jnp.float32,
    ).astype(jnp.bfloat16)
    heads_here = qkv_weight.shape[2] // E
    scale = E ** (-0.25)
    key_part = projected[1].astype(jnp.float32).reshape(tokens, heads_here, E) * scale
    keep = tissue.reshape(tokens).astype(jnp.bfloat16)
    key_feat = features(key_part, omega) * keep[:, None, None]
    value_part = projected[2].reshape(tokens, heads_here, E)
    state = jnp.einsum("the,thm->hem", value_part, key_feat, preferred_element_type=jnp.float32)
    key_sum = jnp.sum(key_feat.astype(jnp.float32), axis=0)
    kv_state, normalizer = lax.psum((state, key_sum), ("tile", "col"))
    query_part = projected[0].astype(jnp.float32).reshape(tokens, heads_here, E) * scale
    query_feat = features(query_part, omega)
    state_upper, state_lower = split_pair(kv_state)
    norm_upper, norm_lower = split_pair(normalizer)
    numer = jnp.einsum("thm,hem->the", query_feat, state_upper, preferred_element_type=jnp.float32)
    numer = numer + jnp.einsum(
        "thm,hem->the", query_feat, state_lower, preferred_element_type=jnp.float32
    )
    denom = jnp.einsum("thm,hm->th", query_feat, norm_upper, preferred_element_type=jnp.float32)
    denom = denom + jnp.einsum(
        "thm,hm->th", query_feat, norm_lower, preferred_element_type=jnp.float32
    )
    attended = (numer / denom[:, :, None]).astype(jnp.bfloat16).reshape(tokens, heads_here * E)
    mixed = (
        lax.psum_scatter(
            lax.dot_general(
                out_weight, attended, (((0,), (1,)), ((), ())), preferred_element_type=jnp.float32
            ).astype(jnp.bfloat16),
            "mp",
            scatter_dimension=0,
            tiled=True,
        )
        .astype(jnp.float32)
        .T
    )
    return (flat + mixed).astype(jnp.bfloat16).reshape(rows_here, cols_here, half)


MESH = pl.DeviceIdType.MESH
F32 = jnp.float32
BF16 = jnp.bfloat16


def remote(src, dst, send, recv, **where):
    return pltpu.make_async_remote_copy(
        src_ref=src, dst_ref=dst, send_sem=send, recv_sem=recv, device_id=where, device_id_type=MESH
    )


def layer_kernel(
    tiles,
    patches_ref,
    tissue_ref,
    conv_ref,
    gain_ref,
    qkv_ref,
    omega_ref,
    outw_ref,
    out_ref,
    pbuf,
    padded,
    rowh,
    colh,
    edge,
    small,
    qkvw,
    wout,
    stem,
    nrm,
    keep,
    lift,
    kbuf,
    vbuf,
    qbuf,
    qfb,
    rs_send,
    rs_recv,
    ag,
    rd,
    att,
    load_sem,
    patch_sem,
    row_ssem,
    row_rsem,
    col_ssem,
    col_rsem,
    small_sem,
    wout_sem,
    rs_ssem,
    rs_rsem,
    ag_ssem,
    ag_rsem,
    att_ssem,
    att_rsem,
):
    rows, cols, half = patches_ref.shape
    tokens = rows * cols
    group = 2 * tiles
    pairs = group // 2
    tile, col, core = lax.axis_index("tile"), lax.axis_index("col"), lax.axis_index("mp")
    me = 2 * tile + col
    other = 1 - core

    local = [
        pltpu.make_async_copy(patches_ref, pbuf.at[core], load_sem.at[0]),
        pltpu.make_async_copy(qkv_ref.at[1], qkvw.at[1], load_sem.at[1]),
        pltpu.make_async_copy(qkv_ref.at[2], qkvw.at[2], load_sem.at[2]),
        pltpu.make_async_copy(qkv_ref.at[0], qkvw.at[0], load_sem.at[3]),
        pltpu.make_async_copy(
            outw_ref.at[:, pl.ds(pl.multiple_of(core * half, half), half)],
            wout.at[core],
            load_sem.at[4],
        ),
    ]
    for copy in local:
        copy.start()

    barrier = pltpu.get_barrier_semaphore()
    for step in range(1, 2 * group):
        peer = lax.rem(2 * me + core + step, 2 * group)
        pl.semaphore_signal(
            barrier,
            inc=1,
            device_id={"tile": peer // 4, "col": lax.rem(peer // 2, 2), "mp": lax.rem(peer, 2)},
            device_id_type=MESH,
        )
    for tap in range(3):
        small[core, 3 * tap : 3 * tap + 3, :] = conv_ref[tap].astype(F32)
    small[core, 9:10, :] = gain_ref[...]
    local[0].wait()
    last = pbuf[core, :, 16:24, :].astype(F32)[:, 7:8, :]
    first = pbuf[core, :, 0:8, :].astype(F32)[:, 0:1, :]
    edge[...] = jnp.where(col == 0, last, first).reshape(rows, half).astype(BF16)
    pl.semaphore_wait(barrier, 2 * group - 1)

    above, below = tile > 0, tile < tiles - 1
    side = {"col": 1 - col}

    def row_copy(way, target):
        return remote(
            patches_ref.at[rows - 1 if way == 0 else 0],
            rowh.at[core, way],
            row_ssem.at[way, target],
            row_rsem.at[core, way],
            tile=tile + (1 if way == 0 else -1),
            mp=core if target == 0 else other,
        )

    def col_copy(way, target):
        return remote(
            edge,
            colh.at[core, way],
            col_ssem.at[way, target],
            col_rsem.at[core, way],
            tile=tile + (0, 1, -1)[way],
            mp=core if target == 0 else other,
            **side,
        )

    for target in range(2):
        for way, there in ((0, below), (1, above)):

            @pl.when(there)
            def _(way=way, target=target):
                row_copy(way, target).start()
                col_copy(way + 1, target).start()

        col_copy(0, target).start()
    patch_copy = remote(patches_ref, pbuf.at[core], patch_sem.at[0], patch_sem.at[1], mp=other)
    patch_copy.start()
    small_copy = remote(small.at[core], small.at[core], small_sem.at[0], small_sem.at[1], mp=other)
    small_copy.start()
    wout_copy = remote(
        outw_ref.at[:, pl.ds(pl.multiple_of(other * half, half), half)],
        wout.at[core],
        wout_sem.at[0],
        wout_sem.at[1],
        mp=other,
    )
    wout_copy.start()

    scaled = (omega_ref[...] * E ** (-0.25)).T
    upper = scaled.astype(BF16)
    lower = (scaled - upper.astype(F32)).astype(BF16)
    sixteenth = jnp.full((E, M), -0.5 * E**-0.5, BF16)
    lift[...] = jnp.zeros_like(lift)
    for part, block in enumerate((upper, lower, sixteenth, sixteenth)):
        for odd in range(2):
            lift[128 * part + E * odd : 128 * part + E * odd + E, M * odd : M * odd + M] = block
    rd[...] = jnp.zeros_like(rd)

    row_of = lax.broadcasted_iota(jnp.int32, (rows, cols, rows), 0)
    row_in = lax.broadcasted_iota(jnp.int32, (rows, cols, rows), 2)
    col_of = lax.broadcasted_iota(jnp.int32, (rows, cols, cols), 1)
    col_in = lax.broadcasted_iota(jnp.int32, (rows, cols, cols), 2)
    pick_row = jnp.where(row_of == row_in, 1.0, 0.0).reshape(tokens, rows).astype(BF16)
    pick_col = jnp.where(col_of == col_in, 1.0, 0.0).reshape(tokens, cols)
    marks = jnp.dot(
        pick_row, tissue_ref[...].astype(F32).astype(BF16), preferred_element_type=F32
    )
    keep[...] = jnp.dot(
        (marks * pick_col).astype(BF16), jnp.ones((cols, 128), BF16), preferred_element_type=F32
    )

    def widen(slot):
        start = pl.multiple_of(slot * half, half)
        padded[1 : rows + 1, 8 : 8 + cols, pl.ds(start, half)] = pbuf[slot].astype(F32)

    widen(core)
    patch_copy.wait_recv()
    widen(other)
    for target in range(2):
        slot = core if target == 0 else other
        lanes = pl.ds(pl.multiple_of(slot * half, half), half)
        remote(
            edge, colh.at[slot, 0], col_ssem.at[0, 0], col_rsem.at[slot, 0], mp=other
        ).wait_recv()
        beside = colh[slot, 0].astype(F32)
        zero = jnp.zeros_like(beside)
        left = jnp.where(col == 1, beside, zero)
        right = jnp.where(col == 0, beside, zero)
        padded[1 : rows + 1, 7:8, lanes] = left.reshape(rows, 1, half)
        padded[1 : rows + 1, 8 + cols : 9 + cols, lanes] = right.reshape(rows, 1, half)
        for way, there in ((0, above), (1, below)):
            line = 0 if way == 0 else rows + 1

            @pl.when(there)
            def _(way=way, slot=slot, lanes=lanes, line=line):
                remote(
                    patches_ref.at[0],
                    rowh.at[slot, way],
                    row_ssem.at[way, 0],
                    row_rsem.at[slot, way],
                    mp=other,
                ).wait_recv()
                remote(
                    edge,
                    colh.at[slot, way + 1],
                    col_ssem.at[0, 0],
                    col_rsem.at[slot, way + 1],
                    mp=other,
                ).wait_recv()
                padded[line, 8 : 8 + cols, lanes] = rowh[slot, way].astype(F32)
                at = rows - 1 if way == 0 else 0
                corner = colh[slot, way + 1].astype(F32)[at : at + 1, :]
                blank = jnp.zeros_like(corner)
                padded[line, 7:8, lanes] = jnp.where(col == 1, corner, blank)
                padded[line, 8 + cols : 9 + cols, lanes] = jnp.where(col == 0, corner, blank)

            @pl.when(jnp.logical_not(there))
            def _(lanes=lanes, line=line):
                padded[line, :, lanes] = jnp.zeros((padded.shape[1], half), F32)

    small_copy.wait_recv()

    def stem_rows(step, carry):
        line = 2 * step
        here = pl.ds(pl.multiple_of(step * 2 * cols, 16), 2 * cols)
        parts = []
        for m in range(2):
            lanes = slice(m * half, m * half + half)
            total = padded[pl.ds(line + 1, 2), 8 : 8 + cols, lanes]
            for a in range(3):
                for b in range(3):
                    total = total + small[m, 3 * a + b : 3 * a + b + 1, :].reshape(
                        1, 1, half
                    ) * padded[pl.ds(line + a, 2), 7 + b : 7 + b + cols, lanes]
            flat = total.reshape(2 * cols, half)
            stem[m, here, :] = flat
            parts.append(flat)
        width = 2 * half
        mean_val = sum(jnp.sum(x, axis=1, keepdims=True) for x in parts) / width
        square = sum(jnp.sum(x * x, axis=1, keepdims=True) for x in parts) / width
        factor = lax.rsqrt(square - mean_val * mean_val + 1e-05)
        for m in range(2):
            nrm[here, m * half : m * half + half] = (
                (parts[m] - mean_val) * factor * small[m, 9:10, :]
            ).astype(BF16)
        return carry

    lax.fori_loop(0, rows // 2, stem_rows, 0)

    def project(c):
        return jnp.dot(nrm[...], qkvw[c], preferred_element_type=F32)

    local[1].wait()
    key = project(1)
    for p in range(pairs):
        kbuf[p] = key[:, 128 * p : 128 * p + 128].astype(BF16)
    local[2].wait()
    value = project(2)
    for p in range(pairs):
        vbuf[p] = (value[:, 128 * p : 128 * p + 128] * keep[...]).astype(BF16)

    def phi(pair):
        wide = pair.astype(F32)
        square = wide * wide
        high = square.astype(BF16)
        low = (square - high.astype(F32)).astype(BF16)
        joined = jnp.concatenate([pair, pair, high, low], axis=1)
        lifted = jnp.dot(joined, lift[...], preferred_element_type=F32)
        return (jnp.exp(lifted) * (1.0 / math.sqrt(M))).astype(BF16)

    def share(h):
        return remote(
            rs_send.at[h],
            rs_recv.at[me],
            rs_ssem.at[h],
            rs_rsem.at[me],
            tile=h // 2,
            col=lax.rem(h, 2),
        )

    def key_pair(step, carry):
        p = lax.rem(step + tile, pairs)
        feat = phi(kbuf[p])
        left = jnp.concatenate([vbuf[p], keep[...].astype(BF16)], axis=1)
        state = lax.dot_general(left, feat, (((0,), (0,)), ((), ())), preferred_element_type=F32)
        for odd in range(2):
            h = 2 * p + odd
            rs_send[h, 0:E, :] = state[E * odd : E * odd + E, M * odd : M * odd + M].astype(BF16)
            rs_send[h, E : E + 16, :] = state[128:144, M * odd : M * odd + M].astype(BF16)

            @pl.when(h != me)
            def _(h=h):
                share(h).start()

        return carry

    lax.fori_loop(0, pairs, key_pair, 0)

    local[3].wait()
    query = project(0)
    for p in range(pairs):
        qbuf[p] = query[:, 128 * p : 128 * p + 128].astype(BF16)

    def query_pair(p, carry):
        qfb[p] = phi(qbuf[p])
        return carry

    lax.fori_loop(0, pairs // 2, query_pair, 0)

    total = rs_send[me].astype(F32)
    for step in range(1, group):
        source = lax.rem(me + step, group)
        remote(
            rs_send.at[0], rs_recv.at[source], rs_ssem.at[0], rs_rsem.at[source], mp=other
        ).wait_recv()
        total = total + rs_recv[source].astype(F32)
    ag[me] = total.astype(BF16)

    def spread(step):
        peer = lax.rem(me + step, group)
        return remote(
            ag.at[me],
            ag.at[me],
            ag_ssem.at[step],
            ag_rsem.at[me],
            tile=peer // 2,
            col=lax.rem(peer, 2),
        )

    for step in range(1, group):
        spread(step).start()

    lax.fori_loop(pairs // 2, pairs, query_pair, 0)

    def att_copy(p):
        return remote(
            att.at[core, p], att.at[core, p], att_ssem.at[p], att_rsem.at[core, p], mp=other
        )

    def read_pair(step, carry):
        p = lax.rem(step + tile, pairs)
        for odd in range(2):
            h = 2 * p + odd

            @pl.when(h != me)
            def _(h=h):
                remote(
                    ag.at[h], ag.at[h], ag_ssem.at[0], ag_rsem.at[h], mp=other
                ).wait_recv()

            rd[E * odd : E * odd + E, M * odd : M * odd + M] = ag[h, 0:E, :]
            norm = ag[h, E : E + 16, :]
            for k in range(4):
                at = 128 + E * odd + 16 * k
                rd[at : at + 16, M * odd : M * odd + M] = norm
        both = lax.dot_general(
            qfb[p], rd[...], (((1,), (1,)), ((), ())), preferred_element_type=F32
        )
        att[core, p] = (both[:, :128] / both[:, 128:]).astype(BF16)
        att_copy(p).start()
        return carry

    lax.fori_loop(0, pairs, read_pair, 0)

    def mix(slot):
        return jnp.dot(
            jnp.concatenate([att[slot, p] for p in range(pairs)], axis=1),
            wout[slot],
            preferred_element_type=F32,
        )

    local[4].wait()
    stem[core] = stem[core] + mix(core)
    wout_copy.wait_recv()
    for p in range(pairs):
        remote(
            att.at[core, p], att.at[other, p], att_ssem.at[p], att_rsem.at[other, p], mp=other
        ).wait_recv()
    result = stem[core] + mix(other)
    out_ref[...] = result.reshape(rows, cols, half).astype(BF16)

    for target in range(2):
        for way, there in ((0, below), (1, above)):

            @pl.when(there)
            def _(way=way, target=target):
                row_copy(way, target).wait_send()
                col_copy(way + 1, target).wait_send()

        col_copy(0, target).wait_send()
    for copy in (patch_copy, small_copy, wout_copy):
        copy.wait_send()

    def drain(h, carry):
        @pl.when(h != me)
        def _():
            share(h).wait_send()

        return carry

    lax.fori_loop(0, group, drain, 0)
    for step in range(1, group):
        spread(step).wait_send()
    for p in range(pairs):
        att_copy(p).wait_send()


def fused(tiles, patches, tissue, conv_weight, ln_gain, qkv_weight, omega, out_weight):
    rows, cols, half = patches.shape
    tokens = rows * cols
    group = 2 * tiles
    pairs = group // 2
    vmem, dma = pltpu.VMEM, pltpu.SemaphoreType.DMA
    anywhere = pl.BlockSpec(memory_space=pl.ANY)
    inside = pl.BlockSpec(memory_space=pltpu.VMEM)
    return pl.pallas_call(
        functools.partial(layer_kernel, tiles),
        out_shape=jax.ShapeDtypeStruct(patches.shape, BF16),
        in_specs=[anywhere, inside, inside, inside, anywhere, inside, anywhere],
        out_specs=inside,
        scratch_shapes=[
            vmem((2, rows, cols, half), BF16),
            vmem((rows + 2, cols + 16, 2 * half), F32),
            vmem((2, 2, cols, half), BF16),
            vmem((2, 3, rows, half), BF16),
            vmem((rows, half), BF16),
            vmem((2, 16, half), F32),
            vmem(qkv_weight.shape, BF16),
            vmem((2, half, half), BF16),
            vmem((2, tokens, half), F32),
            vmem((tokens, 2 * half), BF16),
            vmem((tokens, 128), F32),
            vmem((512, 2 * M), BF16),
            vmem((pairs, tokens, 128), BF16),
            vmem((pairs, tokens, 128), BF16),
            vmem((pairs, tokens, 128), BF16),
            vmem((pairs, tokens, 2 * M), BF16),
            vmem((group, E + 16, M), BF16),
            vmem((group, E + 16, M), BF16),
            vmem((group, E + 16, M), BF16),
            vmem((256, 2 * M), BF16),
            vmem((2, pairs, tokens, 128), BF16),
            dma((5,)),
            dma((2,)),
            dma((2, 2)),
            dma((2, 2)),
            dma((3, 2)),
            dma((2, 3)),
            dma((2,)),
            dma((2,)),
            dma((group,)),
            dma((group,)),
            dma((group,)),
            dma((group,)),
            dma((pairs,)),
            dma((2, pairs)),
        ],
        compiler_params=pltpu.CompilerParams(
            collective_id=0, has_side_effects=True, vmem_limit_bytes=48 * 2**20
        ),
    )(patches, tissue, conv_weight, ln_gain.reshape(1, half), qkv_weight, omega, out_weight)


def solution(mesh):
    tiles, sides, cores = mesh.shape["tile"], mesh.shape["col"], mesh.shape["mp"]

    def body(*args):
        heads_here = args[4].shape[2] // E
        if sides == 2 and cores == 2 and tiles * sides == heads_here:
            return fused(tiles, *args)
        return shards(*args)

    placed = (
        P(("slides", "tile"), "col", "mp"),
        P(("slides", "tile"), "col"),
        P(None, None, "mp"),
        P("mp"),
        P(None, None, "mp"),
        P(),
        P("mp", None),
    )
    return jax.shard_map(
        body,
        mesh=mesh,
        in_specs=placed,
        out_specs=P(("slides", "tile"), "col", "mp"),
        check_vma=False,
    )
```

```python
import functools
import math

import jax
import jax.numpy as jnp
from jax import lax
from jax.experimental import pallas as pl
from jax.experimental.pallas import tpu as pltpu
from jax.sharding import PartitionSpec as P

E = 64
M = 256


def extended(cells, sides, width):
    for axis, dim in sides:
        count = lax.axis_size(axis)
        ends = count - 1
        head = lax.slice_in_dim(cells, 0, width, axis=dim)
        tail = lax.slice_in_dim(cells, cells.shape[dim] - width, cells.shape[dim], axis=dim)
        cells = jnp.concatenate(
            [
                lax.ppermute(tail, axis, [(i, (i + 1) % count) for i in range(ends)]),
                cells,
                lax.ppermute(head, axis, [((i + 1) % count, i) for i in range(ends)]),
            ],
            axis=dim,
        )
    return cells


def features(scaled, omega):
    lifted = jnp.einsum("the,me->thm", scaled, omega, precision=lax.Precision.HIGHEST)
    square = 0.5 * jnp.sum(scaled * scaled, axis=-1, keepdims=True)
    return (jnp.exp(lifted - square) / math.sqrt(M)).astype(jnp.bfloat16)


def split_pair(values):
    upper = values.astype(jnp.bfloat16)
    lower = (values - upper.astype(jnp.float32)).astype(jnp.bfloat16)
    return (upper, lower)


def shards(patches, tissue, conv_weight, ln_gain, qkv_weight, omega, out_weight):
    rows_here, cols_here, half = patches.shape
    tokens = rows_here * cols_here
    padded = extended(patches, (("tile", 0), ("col", 1)), 1)
    widened = padded.astype(jnp.float32)
    kernel = conv_weight.astype(jnp.float32)
    stem = patches.astype(jnp.float32)
    for row_off in range(3):
        for col_off in range(3):
            stem = (
                stem
                + kernel[row_off, col_off]
                * widened[row_off : row_off + rows_here, col_off : col_off + cols_here]
            )
    flat = stem.reshape(tokens, half)
    totals = lax.psum((jnp.sum(flat, axis=1), jnp.sum(flat * flat, axis=1)), "mp")
    width = half * lax.axis_size("mp")
    mean_val = totals[0] / width
    var_val = totals[1] / width - mean_val * mean_val
    normed = ((flat - mean_val[:, None]) * lax.rsqrt(var_val + 1e-05)[:, None] * ln_gain).astype(
        jnp.bfloat16
    )
    projected = jnp.einsum(
        "td,cdf->ctf",
        lax.all_gather(normed, "mp", axis=1, tiled=True),
        qkv_weight,
        preferred_element_type=jnp.float32,
    ).astype(jnp.bfloat16)
    heads_here = qkv_weight.shape[2] // E
    scale = E ** (-0.25)
    key_part = projected[1].astype(jnp.float32).reshape(tokens, heads_here, E) * scale
    keep = tissue.reshape(tokens).astype(jnp.bfloat16)
    key_feat = features(key_part, omega) * keep[:, None, None]
    value_part = projected[2].reshape(tokens, heads_here, E)
    state = jnp.einsum("the,thm->hem", value_part, key_feat, preferred_element_type=jnp.float32)
    key_sum = jnp.sum(key_feat.astype(jnp.float32), axis=0)
    kv_state, normalizer = lax.psum((state, key_sum), ("tile", "col"))
    query_part = projected[0].astype(jnp.float32).reshape(tokens, heads_here, E) * scale
    query_feat = features(query_part, omega)
    state_upper, state_lower = split_pair(kv_state)
    norm_upper, norm_lower = split_pair(normalizer)
    numer = jnp.einsum("thm,hem->the", query_feat, state_upper, preferred_element_type=jnp.float32)
    numer = numer + jnp.einsum(
        "thm,hem->the", query_feat, state_lower, preferred_element_type=jnp.float32
    )
    denom = jnp.einsum("thm,hm->th", query_feat, norm_upper, preferred_element_type=jnp.float32)
    denom = denom + jnp.einsum(
        "thm,hm->th", query_feat, norm_lower, preferred_element_type=jnp.float32
    )
    attended = (numer / denom[:, :, None]).astype(jnp.bfloat16).reshape(tokens, heads_here * E)
    mixed = (
        lax.psum_scatter(
            lax.dot_general(
                out_weight, attended, (((0,), (1,)), ((), ())), preferred_element_type=jnp.float32
            ).astype(jnp.bfloat16),
            "mp",
            scatter_dimension=0,
            tiled=True,
        )
        .astype(jnp.float32)
        .T
    )
    return (flat + mixed).astype(jnp.bfloat16).reshape(rows_here, cols_here, half)


MESH = pl.DeviceIdType.MESH
F32 = jnp.float32
BF16 = jnp.bfloat16


def remote(src, dst, send, recv, **where):
    return pltpu.make_async_remote_copy(
        src_ref=src, dst_ref=dst, send_sem=send, recv_sem=recv, device_id=where, device_id_type=MESH
    )


def layer_kernel(
    tiles,
    patches_ref,
    tissue_hbm,
    conv_hbm,
    gain_hbm,
    qkv_ref,
    omega_hbm,
    outw_ref,
    out_ref,
    tissue_ref,
    conv_ref,
    gain_ref,
    omega_ref,
    pbuf,
    padded,
    rowh,
    colh,
    edge,
    small,
    qkvw,
    wout,
    stem,
    nrm,
    keep,
    lift,
    kbuf,
    vbuf,
    qbuf,
    qfb,
    rs_send,
    xr,
    zs,
    zr,
    ag,
    rd,
    att,
    load_sem,
    patch_sem,
    row_ssem,
    row_rsem,
    col_ssem,
    col_rsem,
    small_sem,
    wout_sem,
    x_ssem,
    x_rsem,
    z_ssem,
    z_rsem,
    ag_ssem,
    fw_ssem,
    ag_rsem,
    att_ssem,
    att_rsem,
):
    rows, cols, half = patches_ref.shape
    tokens = rows * cols
    group = 2 * tiles
    pairs = group // 2
    tile, col, core = lax.axis_index("tile"), lax.axis_index("col"), lax.axis_index("mp")
    me = 2 * tile + col
    other = 1 - core

    local = [
        pltpu.make_async_copy(patches_ref, pbuf.at[core], load_sem.at[0]),
        pltpu.make_async_copy(qkv_ref.at[1], qkvw.at[1], load_sem.at[1]),
        pltpu.make_async_copy(qkv_ref.at[2], qkvw.at[2], load_sem.at[2]),
        pltpu.make_async_copy(qkv_ref.at[0], qkvw.at[0], load_sem.at[3]),
        pltpu.make_async_copy(
            outw_ref.at[:, pl.ds(pl.multiple_of(core * half, half), half)],
            wout.at[core],
            load_sem.at[4],
        ),
        pltpu.make_async_copy(conv_hbm, conv_ref, load_sem.at[5]),
        pltpu.make_async_copy(gain_hbm, gain_ref, load_sem.at[6]),
        pltpu.make_async_copy(omega_hbm, omega_ref, load_sem.at[7]),
        pltpu.make_async_copy(tissue_hbm, tissue_ref, load_sem.at[8]),
    ]
    for index in (0, 5, 6, 7, 8, 1, 2, 3, 4):
        local[index].start()

    barrier = pltpu.get_barrier_semaphore()
    for step in range(1, 2 * group):
        peer = lax.rem(2 * me + core + step, 2 * group)
        pl.semaphore_signal(
            barrier,
            inc=1,
            device_id={"tile": peer // 4, "col": lax.rem(peer // 2, 2), "mp": lax.rem(peer, 2)},
            device_id_type=MESH,
        )
    local[5].wait()
    local[6].wait()
    for tap in range(3):
        small[core, 3 * tap : 3 * tap + 3, :] = conv_ref[tap].astype(F32)
    small[core, 9:10, :] = gain_ref[...]
    local[0].wait()
    last = pbuf[core, :, 16:24, :].astype(F32)[:, 7:8, :]
    first = pbuf[core, :, 0:8, :].astype(F32)[:, 0:1, :]
    edge[...] = jnp.where(col == 0, last, first).reshape(rows, half).astype(BF16)
    pl.semaphore_wait(barrier, 2 * group - 1)

    above, below = tile > 0, tile < tiles - 1
    side = {"col": 1 - col}

    def row_copy(way, target):
        return remote(
            patches_ref.at[rows - 1 if way == 0 else 0],
            rowh.at[core, way],
            row_ssem.at[way, target],
            row_rsem.at[core, way],
            tile=tile + (1 if way == 0 else -1),
            mp=core if target == 0 else other,
        )

    def col_copy(way, target):
        return remote(
            edge,
            colh.at[core, way],
            col_ssem.at[way, target],
            col_rsem.at[core, way],
            tile=tile + (0, 1, -1)[way],
            mp=core if target == 0 else other,
            **side,
        )

    for target in range(2):
        for way, there in ((0, below), (1, above)):

            @pl.when(there)
            def _(way=way, target=target):
                row_copy(way, target).start()
                col_copy(way + 1, target).start()

        col_copy(0, target).start()
    patch_copy = remote(patches_ref, pbuf.at[core], patch_sem.at[0], patch_sem.at[1], mp=other)
    patch_copy.start()
    small_copy = remote(small.at[core], small.at[core], small_sem.at[0], small_sem.at[1], mp=other)
    small_copy.start()
    wout_copy = remote(
        outw_ref.at[:, pl.ds(pl.multiple_of(other * half, half), half)],
        wout.at[core],
        wout_sem.at[0],
        wout_sem.at[1],
        mp=other,
    )
    wout_copy.start()

    local[7].wait()
    scaled = omega_ref[...] * E ** (-0.25)
    upper = scaled.astype(BF16)
    lower = (scaled - upper.astype(F32)).astype(BF16)
    sixteenth = jnp.full((E, M), -0.5 * E**-0.5, BF16)
    lift[...] = jnp.zeros_like(lift)
    for part, block in enumerate((upper, lower, sixteenth, sixteenth)):
        for odd in range(2):
            lift[128 * part + E * odd : 128 * part + E * odd + E, M * odd : M * odd + M] = block
    rd[...] = jnp.zeros_like(rd)

    local[8].wait()
    row_of = lax.broadcasted_iota(jnp.int32, (rows, cols, rows), 0)
    row_in = lax.broadcasted_iota(jnp.int32, (rows, cols, rows), 2)
    col_of = lax.broadcasted_iota(jnp.int32, (rows, cols, cols), 1)
    col_in = lax.broadcasted_iota(jnp.int32, (rows, cols, cols), 2)
    pick_row = jnp.where(row_of == row_in, 1.0, 0.0).reshape(tokens, rows).astype(BF16)
    pick_col = jnp.where(col_of == col_in, 1.0, 0.0).reshape(tokens, cols)
    marks = jnp.dot(
        pick_row, tissue_ref[...].astype(F32).astype(BF16), preferred_element_type=F32
    )
    keep[...] = jnp.dot(
        (marks * pick_col).astype(BF16), jnp.ones((cols, 128), BF16), preferred_element_type=F32
    )

    def widen(slot):
        start = pl.multiple_of(slot * half, half)
        padded[1 : rows + 1, 8 : 8 + cols, pl.ds(start, half)] = pbuf[slot].astype(F32)

    widen(core)
    patch_copy.wait_recv()
    widen(other)
    for target in range(2):
        slot = core if target == 0 else other
        lanes = pl.ds(pl.multiple_of(slot * half, half), half)
        remote(
            edge, colh.at[slot, 0], col_ssem.at[0, 0], col_rsem.at[slot, 0], mp=other
        ).wait_recv()
        beside = colh[slot, 0].astype(F32)
        zero = jnp.zeros_like(beside)
        left = jnp.where(col == 1, beside, zero)
        right = jnp.where(col == 0, beside, zero)
        padded[1 : rows + 1, 7:8, lanes] = left.reshape(rows, 1, half)
        padded[1 : rows + 1, 8 + cols : 9 + cols, lanes] = right.reshape(rows, 1, half)
        for way, there in ((0, above), (1, below)):
            line = 0 if way == 0 else rows + 1

            @pl.when(there)
            def _(way=way, slot=slot, lanes=lanes, line=line):
                remote(
                    patches_ref.at[0],
                    rowh.at[slot, way],
                    row_ssem.at[way, 0],
                    row_rsem.at[slot, way],
                    mp=other,
                ).wait_recv()
                remote(
                    edge,
                    colh.at[slot, way + 1],
                    col_ssem.at[0, 0],
                    col_rsem.at[slot, way + 1],
                    mp=other,
                ).wait_recv()
                padded[line, 8 : 8 + cols, lanes] = rowh[slot, way].astype(F32)
                at = rows - 1 if way == 0 else 0
                corner = colh[slot, way + 1].astype(F32)[at : at + 1, :]
                blank = jnp.zeros_like(corner)
                padded[line, 7:8, lanes] = jnp.where(col == 1, corner, blank)
                padded[line, 8 + cols : 9 + cols, lanes] = jnp.where(col == 0, corner, blank)

            @pl.when(jnp.logical_not(there))
            def _(lanes=lanes, line=line):
                padded[line, :, lanes] = jnp.zeros((padded.shape[1], half), F32)

    small_copy.wait_recv()

    def stem_rows(step, carry):
        line = 2 * step
        here = pl.ds(pl.multiple_of(step * 2 * cols, 16), 2 * cols)
        parts = []
        for m in range(2):
            lanes = slice(m * half, m * half + half)
            total = padded[pl.ds(line + 1, 2), 8 : 8 + cols, lanes]
            for a in range(3):
                for b in range(3):
                    total = total + small[m, 3 * a + b : 3 * a + b + 1, :].reshape(
                        1, 1, half
                    ) * padded[pl.ds(line + a, 2), 7 + b : 7 + b + cols, lanes]
            flat = total.reshape(2 * cols, half)
            stem[m, here, :] = flat
            parts.append(flat)
        width = 2 * half
        mean_val = sum(jnp.sum(x, axis=1, keepdims=True) for x in parts) / width
        square = sum(jnp.sum(x * x, axis=1, keepdims=True) for x in parts) / width
        factor = lax.rsqrt(square - mean_val * mean_val + 1e-05)
        for m in range(2):
            nrm[here, m * half : m * half + half] = (
                (parts[m] - mean_val) * factor * small[m, 9:10, :]
            ).astype(BF16)
        return carry

    lax.fori_loop(0, rows // 2, stem_rows, 0)

    def project(c):
        return jnp.dot(nrm[...], qkvw[c], preferred_element_type=F32)

    local[1].wait()
    key = project(1)
    for p in range(pairs):
        kbuf[p] = key[:, 128 * p : 128 * p + 128].astype(BF16)
    local[2].wait()
    value = project(2)
    for p in range(pairs):
        vbuf[p] = (value[:, 128 * p : 128 * p + 128] * keep[...]).astype(BF16)

    def phi(pair):
        wide = pair.astype(F32)
        square = wide * wide
        high = square.astype(BF16)
        low = (square - high.astype(F32)).astype(BF16)
        joined = jnp.concatenate([pair, pair, high, low], axis=1)
        lifted = jnp.dot(joined, lift[...], preferred_element_type=F32)
        return (jnp.exp(lifted) * (1.0 / math.sqrt(M))).astype(BF16)

    def across(p):
        return remote(
            rs_send.at[2 * p + 1 - col], xr.at[p], x_ssem.at[p], x_rsem.at[p], col=1 - col
        )

    def along(p):
        return remote(zs.at[p], zr.at[tile], z_ssem.at[p], z_rsem.at[tile], tile=p)

    def key_pair(step, carry):
        p = lax.rem(step + 1 + tile, pairs)
        feat = phi(kbuf[p])
        left = jnp.concatenate([vbuf[p], keep[...].astype(BF16)], axis=1)
        state = lax.dot_general(left, feat, (((0,), (0,)), ((), ())), preferred_element_type=F32)
        for odd in range(2):
            h = 2 * p + odd
            rs_send[h, 0:E, :] = state[E * odd : E * odd + E, M * odd : M * odd + M].astype(BF16)
            rs_send[h, E : E + 16, :] = state[128:144, M * odd : M * odd + M].astype(BF16)
        across(p).start()
        return carry

    lax.fori_loop(0, pairs, key_pair, 0)

    local[3].wait()
    query = project(0)
    for p in range(pairs):
        qbuf[p] = query[:, 128 * p : 128 * p + 128].astype(BF16)

    def query_pair(p, carry):
        qfb[p] = phi(qbuf[p])
        return carry


    def fold_pair(step, carry):
        p = lax.rem(step + 1 + tile, pairs)
        across(p).wait_recv()
        zs[p] = (rs_send[2 * p + col].astype(F32) + xr[p].astype(F32)).astype(BF16)

        @pl.when(p != tile)
        def _():
            along(p).start()

        return carry

    lax.fori_loop(0, pairs, fold_pair, 0)
    lax.fori_loop(0, pairs // 2, query_pair, 0)

    total = zs[tile].astype(F32)
    for step in range(1, tiles):
        source = lax.rem(tile + step, tiles)
        remote(
            zs.at[0], zr.at[source], z_ssem.at[0], z_rsem.at[source], mp=other
        ).wait_recv()
        total = total + zr[source].astype(F32)
    ag[me] = total.astype(BF16)

    def spread(step):
        return remote(
            ag.at[me],
            ag.at[me],
            ag_ssem.at[step],
            ag_rsem.at[me],
            tile=lax.rem(tile + step, tiles),
        )

    def forward(p):
        h = 2 * p + col
        return remote(ag.at[h], ag.at[h], fw_ssem.at[p], ag_rsem.at[h], col=1 - col)

    def arrived(h):
        remote(ag.at[h], ag.at[h], ag_ssem.at[0], ag_rsem.at[h], mp=other).wait_recv()

    for step in range(1, tiles):
        spread(step).start()
    forward(tile).start()

    lax.fori_loop(pairs // 2, pairs, query_pair, 0)

    def att_copy(p):
        return remote(
            att.at[core, p], att.at[core, p], att_ssem.at[p], att_rsem.at[core, p], mp=other
        )

    def read_pair(step, carry):
        p = lax.rem(step + tile, pairs)
        later = lax.rem(p + 1, pairs)

        @pl.when(step < pairs - 1)
        def _():
            arrived(2 * later + col)
            forward(later).start()

        arrived(2 * p + 1 - col)
        for odd in range(2):
            h = 2 * p + odd
            rd[E * odd : E * odd + E, M * odd : M * odd + M] = ag[h, 0:E, :]
            norm = ag[h, E : E + 16, :]
            for k in range(4):
                at = 128 + E * odd + 16 * k
                rd[at : at + 16, M * odd : M * odd + M] = norm
        both = lax.dot_general(
            qfb[p], rd[...], (((1,), (1,)), ((), ())), preferred_element_type=F32
        )
        att[core, p] = (both[:, :128] / both[:, 128:]).astype(BF16)
        att_copy(p).start()
        return carry

    lax.fori_loop(0, pairs, read_pair, 0)

    def mix(slot):
        return jnp.dot(
            jnp.concatenate([att[slot, p] for p in range(pairs)], axis=1),
            wout[slot],
            preferred_element_type=F32,
        )

    local[4].wait()
    stem[core] = stem[core] + mix(core)
    wout_copy.wait_recv()
    for p in range(pairs):
        remote(
            att.at[core, p], att.at[other, p], att_ssem.at[p], att_rsem.at[other, p], mp=other
        ).wait_recv()
    result = stem[core] + mix(other)
    out_ref[...] = result.reshape(rows, cols, half).astype(BF16)

    for target in range(2):
        for way, there in ((0, below), (1, above)):

            @pl.when(there)
            def _(way=way, target=target):
                row_copy(way, target).wait_send()
                col_copy(way + 1, target).wait_send()

        col_copy(0, target).wait_send()
    for copy in (patch_copy, small_copy, wout_copy):
        copy.wait_send()

    for step in range(1, tiles):
        spread(step).wait_send()
        along(lax.rem(tile + step, tiles)).wait_send()
    for p in range(pairs):
        across(p).wait_send()
        forward(p).wait_send()
    for p in range(pairs):
        att_copy(p).wait_send()


def fused(tiles, patches, tissue, conv_weight, ln_gain, qkv_weight, omega, out_weight):
    rows, cols, half = patches.shape
    tokens = rows * cols
    group = 2 * tiles
    pairs = group // 2
    vmem, dma = pltpu.VMEM, pltpu.SemaphoreType.DMA
    anywhere = pl.BlockSpec(memory_space=pl.ANY)
    inside = pl.BlockSpec(memory_space=pltpu.VMEM)
    return pl.pallas_call(
        functools.partial(layer_kernel, tiles),
        out_shape=jax.ShapeDtypeStruct(patches.shape, BF16),
        in_specs=[anywhere] * 7,
        out_specs=inside,
        scratch_shapes=[
            vmem(tissue.shape, jnp.int32),
            vmem(conv_weight.shape, BF16),
            vmem((1, half), F32),
            vmem((E, M), F32),
            vmem((2, rows, cols, half), BF16),
            vmem((rows + 2, cols + 16, 2 * half), F32),
            vmem((2, 2, cols, half), BF16),
            vmem((2, 3, rows, half), BF16),
            vmem((rows, half), BF16),
            vmem((2, 16, half), F32),
            vmem(qkv_weight.shape, BF16),
            vmem((2, half, half), BF16),
            vmem((2, tokens, half), F32),
            vmem((tokens, 2 * half), BF16),
            vmem((tokens, 128), F32),
            vmem((512, 2 * M), BF16),
            vmem((pairs, tokens, 128), BF16),
            vmem((pairs, tokens, 128), BF16),
            vmem((pairs, tokens, 128), BF16),
            vmem((pairs, tokens, 2 * M), BF16),
            vmem((group, E + 16, M), BF16),
            vmem((pairs, E + 16, M), BF16),
            vmem((pairs, E + 16, M), BF16),
            vmem((tiles, E + 16, M), BF16),
            vmem((group, E + 16, M), BF16),
            vmem((256, 2 * M), BF16),
            vmem((2, pairs, tokens, 128), BF16),
            dma((9,)),
            dma((2,)),
            dma((2, 2)),
            dma((2, 2)),
            dma((3, 2)),
            dma((2, 3)),
            dma((2,)),
            dma((2,)),
            dma((pairs,)),
            dma((pairs,)),
            dma((pairs,)),
            dma((tiles,)),
            dma((tiles,)),
            dma((pairs,)),
            dma((group,)),
            dma((pairs,)),
            dma((2, pairs)),
        ],
        compiler_params=pltpu.CompilerParams(
            collective_id=0, has_side_effects=True, vmem_limit_bytes=63 * 2**20
        ),
    )(patches, tissue, conv_weight, ln_gain.reshape(1, half), qkv_weight, omega.T, out_weight)


def solution(mesh):
    tiles, sides, cores = mesh.shape["tile"], mesh.shape["col"], mesh.shape["mp"]

    def body(*args):
        heads_here = args[4].shape[2] // E
        if sides == 2 and cores == 2 and tiles * sides == heads_here:
            return fused(tiles, *args)
        return shards(*args)

    placed = (
        P(("slides", "tile"), "col", "mp"),
        P(("slides", "tile"), "col"),
        P(None, None, "mp"),
        P("mp"),
        P(None, None, "mp"),
        P(),
        P("mp", None),
    )
    return jax.shard_map(
        body,
        mesh=mesh,
        in_specs=placed,
        out_specs=P(("slides", "tile"), "col", "mp"),
        check_vma=False,
    )
```

```python
import functools
import math

import jax
import jax.numpy as jnp
from jax import lax
from jax.experimental import pallas as pl
from jax.experimental.pallas import tpu as pltpu
from jax.sharding import PartitionSpec as P

E = 64
M = 256


def extended(cells, sides, width):
    for axis, dim in sides:
        count = lax.axis_size(axis)
        ends = count - 1
        head = lax.slice_in_dim(cells, 0, width, axis=dim)
        tail = lax.slice_in_dim(cells, cells.shape[dim] - width, cells.shape[dim], axis=dim)
        cells = jnp.concatenate(
            [
                lax.ppermute(tail, axis, [(i, (i + 1) % count) for i in range(ends)]),
                cells,
                lax.ppermute(head, axis, [((i + 1) % count, i) for i in range(ends)]),
            ],
            axis=dim,
        )
    return cells


def features(scaled, omega):
    lifted = jnp.einsum("the,me->thm", scaled, omega, precision=lax.Precision.HIGHEST)
    square = 0.5 * jnp.sum(scaled * scaled, axis=-1, keepdims=True)
    return (jnp.exp(lifted - square) / math.sqrt(M)).astype(jnp.bfloat16)


def split_pair(values):
    upper = values.astype(jnp.bfloat16)
    lower = (values - upper.astype(jnp.float32)).astype(jnp.bfloat16)
    return (upper, lower)


def shards(patches, tissue, conv_weight, ln_gain, qkv_weight, omega, out_weight):
    rows_here, cols_here, half = patches.shape
    tokens = rows_here * cols_here
    padded = extended(patches, (("tile", 0), ("col", 1)), 1)
    widened = padded.astype(jnp.float32)
    kernel = conv_weight.astype(jnp.float32)
    stem = patches.astype(jnp.float32)
    for row_off in range(3):
        for col_off in range(3):
            stem = (
                stem
                + kernel[row_off, col_off]
                * widened[row_off : row_off + rows_here, col_off : col_off + cols_here]
            )
    flat = stem.reshape(tokens, half)
    totals = lax.psum((jnp.sum(flat, axis=1), jnp.sum(flat * flat, axis=1)), "mp")
    width = half * lax.axis_size("mp")
    mean_val = totals[0] / width
    var_val = totals[1] / width - mean_val * mean_val
    normed = ((flat - mean_val[:, None]) * lax.rsqrt(var_val + 1e-05)[:, None] * ln_gain).astype(
        jnp.bfloat16
    )
    projected = jnp.einsum(
        "td,cdf->ctf",
        lax.all_gather(normed, "mp", axis=1, tiled=True),
        qkv_weight,
        preferred_element_type=jnp.float32,
    ).astype(jnp.bfloat16)
    heads_here = qkv_weight.shape[2] // E
    scale = E ** (-0.25)
    key_part = projected[1].astype(jnp.float32).reshape(tokens, heads_here, E) * scale
    keep = tissue.reshape(tokens).astype(jnp.bfloat16)
    key_feat = features(key_part, omega) * keep[:, None, None]
    value_part = projected[2].reshape(tokens, heads_here, E)
    state = jnp.einsum("the,thm->hem", value_part, key_feat, preferred_element_type=jnp.float32)
    key_sum = jnp.sum(key_feat.astype(jnp.float32), axis=0)
    kv_state, normalizer = lax.psum((state, key_sum), ("tile", "col"))
    query_part = projected[0].astype(jnp.float32).reshape(tokens, heads_here, E) * scale
    query_feat = features(query_part, omega)
    state_upper, state_lower = split_pair(kv_state)
    norm_upper, norm_lower = split_pair(normalizer)
    numer = jnp.einsum("thm,hem->the", query_feat, state_upper, preferred_element_type=jnp.float32)
    numer = numer + jnp.einsum(
        "thm,hem->the", query_feat, state_lower, preferred_element_type=jnp.float32
    )
    denom = jnp.einsum("thm,hm->th", query_feat, norm_upper, preferred_element_type=jnp.float32)
    denom = denom + jnp.einsum(
        "thm,hm->th", query_feat, norm_lower, preferred_element_type=jnp.float32
    )
    attended = (numer / denom[:, :, None]).astype(jnp.bfloat16).reshape(tokens, heads_here * E)
    mixed = (
        lax.psum_scatter(
            lax.dot_general(
                out_weight, attended, (((0,), (1,)), ((), ())), preferred_element_type=jnp.float32
            ).astype(jnp.bfloat16),
            "mp",
            scatter_dimension=0,
            tiled=True,
        )
        .astype(jnp.float32)
        .T
    )
    return (flat + mixed).astype(jnp.bfloat16).reshape(rows_here, cols_here, half)


MESH = pl.DeviceIdType.MESH
F32 = jnp.float32
BF16 = jnp.bfloat16


def remote(src, dst, send, recv, **where):
    return pltpu.make_async_remote_copy(
        src_ref=src, dst_ref=dst, send_sem=send, recv_sem=recv, device_id=where, device_id_type=MESH
    )


def layer_kernel(
    tiles,
    patches_ref,
    tissue_hbm,
    conv_hbm,
    gain_hbm,
    qkv_ref,
    omega_hbm,
    outw_ref,
    out_ref,
    tissue_ref,
    conv_ref,
    gain_ref,
    omega_ref,
    pbuf,
    padded,
    rowh,
    colh,
    edge,
    small,
    qkvw,
    wout,
    stem,
    nrm,
    keep,
    lift,
    kbuf,
    vbuf,
    qbuf,
    qfb,
    rs_send,
    rs_recv,
    ag,
    norms,
    norms_all,
    rd,
    att,
    load_sem,
    patch_sem,
    row_ssem,
    row_rsem,
    col_ssem,
    col_rsem,
    small_sem,
    wout_sem,
    rs_ssem,
    rs_rsem,
    ag_ssem,
    ag_rsem,
    att_ssem,
    att_rsem,
    nz_ssem,
    nz_rsem,
):
    rows, cols, half = patches_ref.shape
    tokens = rows * cols
    group = 2 * tiles
    pairs = group // 2
    tile, col, core = lax.axis_index("tile"), lax.axis_index("col"), lax.axis_index("mp")
    me = 2 * tile + col
    other = 1 - core

    local = [
        pltpu.make_async_copy(patches_ref, pbuf.at[core], load_sem.at[0]),
        pltpu.make_async_copy(qkv_ref.at[1], qkvw.at[1], load_sem.at[1]),
        pltpu.make_async_copy(qkv_ref.at[2], qkvw.at[2], load_sem.at[2]),
        pltpu.make_async_copy(qkv_ref.at[0], qkvw.at[0], load_sem.at[3]),
        pltpu.make_async_copy(
            outw_ref.at[:, pl.ds(pl.multiple_of(core * half, half), half)],
            wout.at[core],
            load_sem.at[4],
        ),
        pltpu.make_async_copy(conv_hbm, conv_ref, load_sem.at[5]),
        pltpu.make_async_copy(gain_hbm, gain_ref, load_sem.at[6]),
        pltpu.make_async_copy(omega_hbm, omega_ref, load_sem.at[7]),
        pltpu.make_async_copy(tissue_hbm, tissue_ref, load_sem.at[8]),
    ]
    for index in (0, 5, 6, 7, 8, 1, 2, 3, 4):
        local[index].start()

    barrier = pltpu.get_barrier_semaphore()
    for step in range(1, 2 * group):
        peer = lax.rem(2 * me + core + step, 2 * group)
        pl.semaphore_signal(
            barrier,
            inc=1,
            device_id={"tile": peer // 4, "col": lax.rem(peer // 2, 2), "mp": lax.rem(peer, 2)},
            device_id_type=MESH,
        )
    local[5].wait()
    local[6].wait()
    for tap in range(3):
        small[core, 3 * tap : 3 * tap + 3, :] = conv_ref[tap].astype(F32)
    small[core, 9:10, :] = gain_ref[...]
    local[0].wait()
    last = pbuf[core, :, 16:24, :].astype(F32)[:, 7:8, :]
    first = pbuf[core, :, 0:8, :].astype(F32)[:, 0:1, :]
    edge[...] = jnp.where(col == 0, last, first).reshape(rows, half).astype(BF16)
    pl.semaphore_wait(barrier, 2 * group - 1)

    above, below = tile > 0, tile < tiles - 1
    side = {"col": 1 - col}

    def row_copy(way, target):
        return remote(
            patches_ref.at[rows - 1 if way == 0 else 0],
            rowh.at[core, way],
            row_ssem.at[way, target],
            row_rsem.at[core, way],
            tile=tile + (1 if way == 0 else -1),
            mp=core if target == 0 else other,
        )

    def col_copy(way, target):
        return remote(
            edge,
            colh.at[core, way],
            col_ssem.at[way, target],
            col_rsem.at[core, way],
            tile=tile + (0, 1, -1)[way],
            mp=core if target == 0 else other,
            **side,
        )

    for target in range(2):
        for way, there in ((0, below), (1, above)):

            @pl.when(there)
            def _(way=way, target=target):
                row_copy(way, target).start()
                col_copy(way + 1, target).start()

        col_copy(0, target).start()
    patch_copy = remote(patches_ref, pbuf.at[core], patch_sem.at[0], patch_sem.at[1], mp=other)
    patch_copy.start()
    small_copy = remote(small.at[core], small.at[core], small_sem.at[0], small_sem.at[1], mp=other)
    small_copy.start()
    wout_copy = remote(
        outw_ref.at[:, pl.ds(pl.multiple_of(other * half, half), half)],
        wout.at[core],
        wout_sem.at[0],
        wout_sem.at[1],
        mp=other,
    )
    wout_copy.start()

    local[7].wait()
    scaled = omega_ref[...] * E ** (-0.25)
    upper = scaled.astype(BF16)
    lower = (scaled - upper.astype(F32)).astype(BF16)
    sixteenth = jnp.full((E, M), -0.5 * E**-0.5, BF16)
    lift[...] = jnp.zeros_like(lift)
    for part, block in enumerate((upper, lower, sixteenth, sixteenth)):
        for odd in range(2):
            lift[128 * part + E * odd : 128 * part + E * odd + E, M * odd : M * odd + M] = block
    rd[...] = jnp.zeros_like(rd)

    local[8].wait()
    row_of = lax.broadcasted_iota(jnp.int32, (rows, cols, rows), 0)
    row_in = lax.broadcasted_iota(jnp.int32, (rows, cols, rows), 2)
    col_of = lax.broadcasted_iota(jnp.int32, (rows, cols, cols), 1)
    col_in = lax.broadcasted_iota(jnp.int32, (rows, cols, cols), 2)
    pick_row = jnp.where(row_of == row_in, 1.0, 0.0).reshape(tokens, rows).astype(BF16)
    pick_col = jnp.where(col_of == col_in, 1.0, 0.0).reshape(tokens, cols)
    marks = jnp.dot(
        pick_row, tissue_ref[...].astype(F32).astype(BF16), preferred_element_type=F32
    )
    keep[...] = jnp.dot(
        (marks * pick_col).astype(BF16), jnp.ones((cols, 128), BF16), preferred_element_type=F32
    )

    def widen(slot):
        start = pl.multiple_of(slot * half, half)
        padded[1 : rows + 1, 8 : 8 + cols, pl.ds(start, half)] = pbuf[slot].astype(F32)

    widen(core)
    patch_copy.wait_recv()
    widen(other)
    for target in range(2):
        slot = core if target == 0 else other
        lanes = pl.ds(pl.multiple_of(slot * half, half), half)
        remote(
            edge, colh.at[slot, 0], col_ssem.at[0, 0], col_rsem.at[slot, 0], mp=other
        ).wait_recv()
        beside = colh[slot, 0].astype(F32)
        zero = jnp.zeros_like(beside)
        left = jnp.where(col == 1, beside, zero)
        right = jnp.where(col == 0, beside, zero)
        padded[1 : rows + 1, 7:8, lanes] = left.reshape(rows, 1, half)
        padded[1 : rows + 1, 8 + cols : 9 + cols, lanes] = right.reshape(rows, 1, half)
        for way, there in ((0, above), (1, below)):
            line = 0 if way == 0 else rows + 1

            @pl.when(there)
            def _(way=way, slot=slot, lanes=lanes, line=line):
                remote(
                    patches_ref.at[0],
                    rowh.at[slot, way],
                    row_ssem.at[way, 0],
                    row_rsem.at[slot, way],
                    mp=other,
                ).wait_recv()
                remote(
                    edge,
                    colh.at[slot, way + 1],
                    col_ssem.at[0, 0],
                    col_rsem.at[slot, way + 1],
                    mp=other,
                ).wait_recv()
                padded[line, 8 : 8 + cols, lanes] = rowh[slot, way].astype(F32)
                at = rows - 1 if way == 0 else 0
                corner = colh[slot, way + 1].astype(F32)[at : at + 1, :]
                blank = jnp.zeros_like(corner)
                padded[line, 7:8, lanes] = jnp.where(col == 1, corner, blank)
                padded[line, 8 + cols : 9 + cols, lanes] = jnp.where(col == 0, corner, blank)

            @pl.when(jnp.logical_not(there))
            def _(lanes=lanes, line=line):
                padded[line, :, lanes] = jnp.zeros((padded.shape[1], half), F32)

    small_copy.wait_recv()

    def stem_rows(step, carry):
        line = 2 * step
        here = pl.ds(pl.multiple_of(step * 2 * cols, 16), 2 * cols)
        parts = []
        for m in range(2):
            lanes = slice(m * half, m * half + half)
            total = padded[pl.ds(line + 1, 2), 8 : 8 + cols, lanes]
            for a in range(3):
                for b in range(3):
                    total = total + small[m, 3 * a + b : 3 * a + b + 1, :].reshape(
                        1, 1, half
                    ) * padded[pl.ds(line + a, 2), 7 + b : 7 + b + cols, lanes]
            flat = total.reshape(2 * cols, half)
            stem[m, here, :] = flat
            parts.append(flat)
        width = 2 * half
        mean_val = sum(jnp.sum(x, axis=1, keepdims=True) for x in parts) / width
        square = sum(jnp.sum(x * x, axis=1, keepdims=True) for x in parts) / width
        factor = lax.rsqrt(square - mean_val * mean_val + 1e-05)
        for m in range(2):
            nrm[here, m * half : m * half + half] = (
                (parts[m] - mean_val) * factor * small[m, 9:10, :]
            ).astype(BF16)
        return carry

    lax.fori_loop(0, rows // 2, stem_rows, 0)

    def project(c):
        return jnp.dot(nrm[...], qkvw[c], preferred_element_type=F32)

    local[1].wait()
    key = project(1)
    for p in range(pairs):
        kbuf[p] = key[:, 128 * p : 128 * p + 128].astype(BF16)
    local[2].wait()
    value = project(2)
    for p in range(pairs):
        vbuf[p] = (value[:, 128 * p : 128 * p + 128] * keep[...]).astype(BF16)

    def phi(pair):
        wide = pair.astype(F32)
        square = wide * wide
        high = square.astype(BF16)
        low = (square - high.astype(F32)).astype(BF16)
        joined = jnp.concatenate([pair, pair, high, low], axis=1)
        lifted = jnp.dot(joined, lift[...], preferred_element_type=F32)
        return (jnp.exp(lifted) * (1.0 / math.sqrt(M))).astype(BF16)

    def share(h):
        return remote(
            rs_send.at[h],
            rs_recv.at[me],
            rs_ssem.at[h],
            rs_rsem.at[me],
            tile=h // 2,
            col=lax.rem(h, 2),
        )

    def key_pair(step, carry):
        p = lax.rem(step + 1 + tile, pairs)
        feat = phi(kbuf[p])
        left = jnp.concatenate([vbuf[p], keep[...].astype(BF16)], axis=1)
        state = lax.dot_general(left, feat, (((0,), (0,)), ((), ())), preferred_element_type=F32)
        for odd in range(2):
            h = 2 * p + odd
            rs_send[h] = state[E * odd : E * odd + E, M * odd : M * odd + M].astype(BF16)
            norms[pl.ds(h, 1), :] = state[128:129, M * odd : M * odd + M]

            @pl.when(h != me)
            def _(h=h):
                share(h).start()

        return carry

    lax.fori_loop(0, pairs, key_pair, 0)
    norms_all[me] = norms[...]

    def norm_share(step):
        peer = lax.rem(me + step, group)
        return remote(
            norms_all.at[me],
            norms_all.at[me],
            nz_ssem.at[step],
            nz_rsem.at[me],
            tile=peer // 2,
            col=lax.rem(peer, 2),
        )

    for step in range(1, group):
        norm_share(step).start()
    local[3].wait()
    query = project(0)
    for p in range(pairs):
        qbuf[p] = query[:, 128 * p : 128 * p + 128].astype(BF16)

    def query_pair(p, carry):
        qfb[p] = phi(qbuf[p])
        return carry


    lax.fori_loop(0, pairs - 1, query_pair, 0)

    total = rs_send[me].astype(F32)
    for step in range(1, group):
        source = lax.rem(me + step, group)
        remote(
            rs_send.at[0], rs_recv.at[source], rs_ssem.at[0], rs_rsem.at[source], mp=other
        ).wait_recv()
        total = total + rs_recv[source].astype(F32)
    ag[me] = total.astype(BF16)

    def spread(step):
        peer = lax.rem(me + step, group)
        return remote(
            ag.at[me],
            ag.at[me],
            ag_ssem.at[step],
            ag_rsem.at[me],
            tile=peer // 2,
            col=lax.rem(peer, 2),
        )

    def arrived(h):
        remote(ag.at[h], ag.at[h], ag_ssem.at[0], ag_rsem.at[h], mp=other).wait_recv()

    for step in range(1, group):
        spread(step).start()

    query_pair(pairs - 1, 0)
    for step in range(1, group):
        source = lax.rem(me + step, group)
        remote(
            norms_all.at[0], norms_all.at[source], nz_ssem.at[0], nz_rsem.at[source], mp=other
        ).wait_recv()
    norms[...] = sum(norms_all[s] for s in range(group))

    def att_copy(p):
        return remote(
            att.at[core, p], att.at[core, p], att_ssem.at[p], att_rsem.at[core, p], mp=other
        )

    def read_pair(step, carry):
        p = lax.rem(step + tile, pairs)
        for odd in range(2):
            h = 2 * p + odd

            @pl.when(h != me)
            def _(h=h):
                arrived(h)

            rd[E * odd : E * odd + E, M * odd : M * odd + M] = ag[h]
            rd[128 + E * odd : 128 + E * odd + E, M * odd : M * odd + M] = jnp.broadcast_to(
                norms[pl.ds(h, 1), :], (E, M)
            ).astype(BF16)
        both = lax.dot_general(
            qfb[p], rd[...], (((1,), (1,)), ((), ())), preferred_element_type=F32
        )
        att[core, p] = (both[:, :128] / both[:, 128:]).astype(BF16)
        att_copy(p).start()
        return carry

    lax.fori_loop(0, pairs, read_pair, 0)

    def mix(slot):
        return jnp.dot(
            jnp.concatenate([att[slot, p] for p in range(pairs)], axis=1),
            wout[slot],
            preferred_element_type=F32,
        )

    local[4].wait()
    stem[core] = stem[core] + mix(core)
    wout_copy.wait_recv()
    for p in range(pairs):
        remote(
            att.at[core, p], att.at[other, p], att_ssem.at[p], att_rsem.at[other, p], mp=other
        ).wait_recv()
    result = stem[core] + mix(other)
    out_ref[...] = result.reshape(rows, cols, half).astype(BF16)

    for target in range(2):
        for way, there in ((0, below), (1, above)):

            @pl.when(there)
            def _(way=way, target=target):
                row_copy(way, target).wait_send()
                col_copy(way + 1, target).wait_send()

        col_copy(0, target).wait_send()
    for copy in (patch_copy, small_copy, wout_copy):
        copy.wait_send()

    def drain(h, carry):
        @pl.when(h != me)
        def _():
            share(h).wait_send()

        return carry

    lax.fori_loop(0, group, drain, 0)
    for step in range(1, group):
        spread(step).wait_send()
        norm_share(step).wait_send()
    for p in range(pairs):
        att_copy(p).wait_send()


def fused(tiles, patches, tissue, conv_weight, ln_gain, qkv_weight, omega, out_weight):
    rows, cols, half = patches.shape
    tokens = rows * cols
    group = 2 * tiles
    pairs = group // 2
    vmem, dma = pltpu.VMEM, pltpu.SemaphoreType.DMA
    anywhere = pl.BlockSpec(memory_space=pl.ANY)
    inside = pl.BlockSpec(memory_space=pltpu.VMEM)
    return pl.pallas_call(
        functools.partial(layer_kernel, tiles),
        out_shape=pltpu.VMEM(patches.shape, BF16),
        in_specs=[anywhere] * 7,
        out_specs=inside,
        scratch_shapes=[
            vmem(tissue.shape, jnp.int32),
            vmem(conv_weight.shape, BF16),
            vmem((1, half), F32),
            vmem((E, M), F32),
            vmem((2, rows, cols, half), BF16),
            vmem((rows + 2, cols + 16, 2 * half), F32),
            vmem((2, 2, cols, half), BF16),
            vmem((2, 3, rows, half), BF16),
            vmem((rows, half), BF16),
            vmem((2, 16, half), F32),
            vmem(qkv_weight.shape, BF16),
            vmem((2, half, half), BF16),
            vmem((2, tokens, half), F32),
            vmem((tokens, 2 * half), BF16),
            vmem((tokens, 128), F32),
            vmem((512, 2 * M), BF16),
            vmem((pairs, tokens, 128), BF16),
            vmem((pairs, tokens, 128), BF16),
            vmem((pairs, tokens, 128), BF16),
            vmem((pairs, tokens, 2 * M), BF16),
            vmem((group, E, M), BF16),
            vmem((group, E, M), BF16),
            vmem((group, E, M), BF16),
            vmem((group, M), F32),
            vmem((group, group, M), F32),
            vmem((256, 2 * M), BF16),
            vmem((2, pairs, tokens, 128), BF16),
            dma((9,)),
            dma((2,)),
            dma((2, 2)),
            dma((2, 2)),
            dma((3, 2)),
            dma((2, 3)),
            dma((2,)),
            dma((2,)),
            dma((group,)),
            dma((group,)),
            dma((group,)),
            dma((group,)),
            dma((pairs,)),
            dma((2, pairs)),
            dma((group,)),
            dma((group,)),
        ],
        compiler_params=pltpu.CompilerParams(
            collective_id=0, has_side_effects=True, vmem_limit_bytes=63 * 2**20
        ),
    )(patches, tissue, conv_weight, ln_gain.reshape(1, half), qkv_weight, omega.T, out_weight)


def solution(mesh):
    tiles, sides, cores = mesh.shape["tile"], mesh.shape["col"], mesh.shape["mp"]

    def body(*args):
        heads_here = args[4].shape[2] // E
        if sides == 2 and cores == 2 and tiles * sides == heads_here:
            return fused(tiles, *args)
        return shards(*args)

    placed = (
        P(("slides", "tile"), "col", "mp"),
        P(("slides", "tile"), "col"),
        P(None, None, "mp"),
        P("mp"),
        P(None, None, "mp"),
        P(),
        P("mp", None),
    )
    return jax.shard_map(
        body,
        mesh=mesh,
        in_specs=placed,
        out_specs=P(("slides", "tile"), "col", "mp"),
        check_vma=False,
    )
```

```python
import functools
import math

import jax
import jax.numpy as jnp
from jax import lax
from jax.experimental import pallas as pl
from jax.experimental.pallas import tpu as pltpu
from jax.sharding import PartitionSpec as P

E = 64
M = 256


def extended(cells, sides, width):
    for axis, dim in sides:
        count = lax.axis_size(axis)
        ends = count - 1
        head = lax.slice_in_dim(cells, 0, width, axis=dim)
        tail = lax.slice_in_dim(cells, cells.shape[dim] - width, cells.shape[dim], axis=dim)
        cells = jnp.concatenate(
            [
                lax.ppermute(tail, axis, [(i, (i + 1) % count) for i in range(ends)]),
                cells,
                lax.ppermute(head, axis, [((i + 1) % count, i) for i in range(ends)]),
            ],
            axis=dim,
        )
    return cells


def features(scaled, omega):
    lifted = jnp.einsum("the,me->thm", scaled, omega, precision=lax.Precision.HIGHEST)
    square = 0.5 * jnp.sum(scaled * scaled, axis=-1, keepdims=True)
    return (jnp.exp(lifted - square) / math.sqrt(M)).astype(jnp.bfloat16)


def split_pair(values):
    upper = values.astype(jnp.bfloat16)
    lower = (values - upper.astype(jnp.float32)).astype(jnp.bfloat16)
    return (upper, lower)


def shards(patches, tissue, conv_weight, ln_gain, qkv_weight, omega, out_weight):
    rows_here, cols_here, half = patches.shape
    tokens = rows_here * cols_here
    padded = extended(patches, (("tile", 0), ("col", 1)), 1)
    widened = padded.astype(jnp.float32)
    kernel = conv_weight.astype(jnp.float32)
    stem = patches.astype(jnp.float32)
    for row_off in range(3):
        for col_off in range(3):
            stem = (
                stem
                + kernel[row_off, col_off]
                * widened[row_off : row_off + rows_here, col_off : col_off + cols_here]
            )
    flat = stem.reshape(tokens, half)
    totals = lax.psum((jnp.sum(flat, axis=1), jnp.sum(flat * flat, axis=1)), "mp")
    width = half * lax.axis_size("mp")
    mean_val = totals[0] / width
    var_val = totals[1] / width - mean_val * mean_val
    normed = ((flat - mean_val[:, None]) * lax.rsqrt(var_val + 1e-05)[:, None] * ln_gain).astype(
        jnp.bfloat16
    )
    projected = jnp.einsum(
        "td,cdf->ctf",
        lax.all_gather(normed, "mp", axis=1, tiled=True),
        qkv_weight,
        preferred_element_type=jnp.float32,
    ).astype(jnp.bfloat16)
    heads_here = qkv_weight.shape[2] // E
    scale = E ** (-0.25)
    key_part = projected[1].astype(jnp.float32).reshape(tokens, heads_here, E) * scale
    keep = tissue.reshape(tokens).astype(jnp.bfloat16)
    key_feat = features(key_part, omega) * keep[:, None, None]
    value_part = projected[2].reshape(tokens, heads_here, E)
    state = jnp.einsum("the,thm->hem", value_part, key_feat, preferred_element_type=jnp.float32)
    key_sum = jnp.sum(key_feat.astype(jnp.float32), axis=0)
    kv_state, normalizer = lax.psum((state, key_sum), ("tile", "col"))
    query_part = projected[0].astype(jnp.float32).reshape(tokens, heads_here, E) * scale
    query_feat = features(query_part, omega)
    state_upper, state_lower = split_pair(kv_state)
    norm_upper, norm_lower = split_pair(normalizer)
    numer = jnp.einsum("thm,hem->the", query_feat, state_upper, preferred_element_type=jnp.float32)
    numer = numer + jnp.einsum(
        "thm,hem->the", query_feat, state_lower, preferred_element_type=jnp.float32
    )
    denom = jnp.einsum("thm,hm->th", query_feat, norm_upper, preferred_element_type=jnp.float32)
    denom = denom + jnp.einsum(
        "thm,hm->th", query_feat, norm_lower, preferred_element_type=jnp.float32
    )
    attended = (numer / denom[:, :, None]).astype(jnp.bfloat16).reshape(tokens, heads_here * E)
    mixed = (
        lax.psum_scatter(
            lax.dot_general(
                out_weight, attended, (((0,), (1,)), ((), ())), preferred_element_type=jnp.float32
            ).astype(jnp.bfloat16),
            "mp",
            scatter_dimension=0,
            tiled=True,
        )
        .astype(jnp.float32)
        .T
    )
    return (flat + mixed).astype(jnp.bfloat16).reshape(rows_here, cols_here, half)


MESH = pl.DeviceIdType.MESH
F32 = jnp.float32
BF16 = jnp.bfloat16


def remote(src, dst, send, recv, **where):
    return pltpu.make_async_remote_copy(
        src_ref=src, dst_ref=dst, send_sem=send, recv_sem=recv, device_id=where, device_id_type=MESH
    )


def layer_kernel(
    tiles,
    patches_ref,
    tissue_hbm,
    conv_hbm,
    gain_hbm,
    qkv_ref,
    omega_hbm,
    outw_ref,
    out_ref,
    tissue_ref,
    conv_ref,
    gain_ref,
    omega_ref,
    pbuf,
    padded,
    rowh,
    colh,
    edge,
    corners,
    cornh,
    small,
    qkvw,
    wout,
    stem,
    nrm,
    keep,
    lift,
    kbuf,
    vbuf,
    qbuf,
    qfb,
    rs_send,
    rs_recv,
    ag,
    norms,
    norms_all,
    rd,
    att,
    load_sem,
    patch_sem,
    row_ssem,
    row_rsem,
    col_ssem,
    col_rsem,
    small_sem,
    wout_sem,
    rs_ssem,
    rs_rsem,
    ag_ssem,
    ag_rsem,
    att_ssem,
    att_rsem,
    nz_ssem,
    nz_rsem,
):
    rows, cols, half = patches_ref.shape
    tokens = rows * cols
    group = 2 * tiles
    pairs = group // 2
    tile, col, core = lax.axis_index("tile"), lax.axis_index("col"), lax.axis_index("mp")
    me = 2 * tile + col
    other = 1 - core

    local = [
        pltpu.make_async_copy(patches_ref, pbuf.at[core], load_sem.at[0]),
        pltpu.make_async_copy(qkv_ref.at[1], qkvw.at[1], load_sem.at[1]),
        pltpu.make_async_copy(qkv_ref.at[2], qkvw.at[2], load_sem.at[2]),
        pltpu.make_async_copy(qkv_ref.at[0], qkvw.at[0], load_sem.at[3]),
        pltpu.make_async_copy(
            outw_ref.at[:, pl.ds(pl.multiple_of(core * half, half), half)],
            wout.at[core],
            load_sem.at[4],
        ),
        pltpu.make_async_copy(conv_hbm, conv_ref, load_sem.at[5]),
        pltpu.make_async_copy(gain_hbm, gain_ref, load_sem.at[6]),
        pltpu.make_async_copy(omega_hbm, omega_ref, load_sem.at[7]),
        pltpu.make_async_copy(tissue_hbm, tissue_ref, load_sem.at[8]),
    ]
    for index in (0, 5, 6, 7, 8, 1, 2, 3, 4):
        local[index].start()

    barrier = pltpu.get_barrier_semaphore()
    for step in range(1, 2 * group):
        peer = lax.rem(2 * me + core + step, 2 * group)
        pl.semaphore_signal(
            barrier,
            inc=1,
            device_id={"tile": peer // 4, "col": lax.rem(peer // 2, 2), "mp": lax.rem(peer, 2)},
            device_id_type=MESH,
        )
    local[5].wait()
    local[6].wait()
    for tap in range(3):
        small[core, 3 * tap : 3 * tap + 3, :] = conv_ref[tap].astype(F32)
    small[core, 9:10, :] = gain_ref[...]
    local[0].wait()
    last = pbuf[core, :, 16:24, :].astype(F32)[:, 7:8, :]
    first = pbuf[core, :, 0:8, :].astype(F32)[:, 0:1, :]
    border = jnp.where(col == 0, last, first).reshape(rows, half)
    edge[...] = border.astype(BF16)
    for way, line in ((0, rows - 1), (1, 0)):
        pieces = [border[line : line + 1, at : at + 128] for at in range(0, half, 128)]
        blank = jnp.zeros((16 - len(pieces), 128), F32)
        corners[way] = jnp.concatenate(pieces + [blank], axis=0).astype(BF16)
    pl.semaphore_wait(barrier, 2 * group - 1)

    above, below = tile > 0, tile < tiles - 1
    side = {"col": 1 - col}

    def row_copy(way, target):
        return remote(
            patches_ref.at[rows - 1 if way == 0 else 0],
            rowh.at[core, way],
            row_ssem.at[way, target],
            row_rsem.at[core, way],
            tile=tile + (1 if way == 0 else -1),
            mp=core if target == 0 else other,
        )

    def col_copy(way, target):
        return remote(
            edge if way == 0 else corners.at[way - 1],
            colh.at[core] if way == 0 else cornh.at[core, way - 1],
            col_ssem.at[way, target],
            col_rsem.at[core, way],
            tile=tile + (0, 1, -1)[way],
            mp=core if target == 0 else other,
            **side,
        )

    for target in range(2):
        for way, there in ((0, below), (1, above)):

            @pl.when(there)
            def _(way=way, target=target):
                row_copy(way, target).start()
                col_copy(way + 1, target).start()

        col_copy(0, target).start()
    patch_copy = remote(patches_ref, pbuf.at[core], patch_sem.at[0], patch_sem.at[1], mp=other)
    patch_copy.start()
    small_copy = remote(small.at[core], small.at[core], small_sem.at[0], small_sem.at[1], mp=other)
    small_copy.start()
    wout_copy = remote(
        outw_ref.at[:, pl.ds(pl.multiple_of(other * half, half), half)],
        wout.at[core],
        wout_sem.at[0],
        wout_sem.at[1],
        mp=other,
    )
    wout_copy.start()

    local[7].wait()
    scaled = omega_ref[...] * E ** (-0.25)
    upper = scaled.astype(BF16)
    lower = (scaled - upper.astype(F32)).astype(BF16)
    sixteenth = jnp.full((E, M), -0.5 * E**-0.5, BF16)
    lift[...] = jnp.zeros_like(lift)
    for part, block in enumerate((upper, lower, sixteenth, sixteenth)):
        for odd in range(2):
            lift[128 * part + E * odd : 128 * part + E * odd + E, M * odd : M * odd + M] = block
    rd[...] = jnp.zeros_like(rd)

    local[8].wait()
    row_of = lax.broadcasted_iota(jnp.int32, (rows, cols, rows), 0)
    row_in = lax.broadcasted_iota(jnp.int32, (rows, cols, rows), 2)
    col_of = lax.broadcasted_iota(jnp.int32, (rows, cols, cols), 1)
    col_in = lax.broadcasted_iota(jnp.int32, (rows, cols, cols), 2)
    pick_row = jnp.where(row_of == row_in, 1.0, 0.0).reshape(tokens, rows).astype(BF16)
    pick_col = jnp.where(col_of == col_in, 1.0, 0.0).reshape(tokens, cols)
    marks = jnp.dot(
        pick_row, tissue_ref[...].astype(F32).astype(BF16), preferred_element_type=F32
    )
    keep[...] = jnp.dot(
        (marks * pick_col).astype(BF16), jnp.ones((cols, 128), BF16), preferred_element_type=F32
    )

    def widen(slot):
        start = pl.multiple_of(slot * half, half)
        padded[1 : rows + 1, 8 : 8 + cols, pl.ds(start, half)] = pbuf[slot].astype(F32)

    widen(core)
    patch_copy.wait_recv()
    widen(other)
    for target in range(2):
        slot = core if target == 0 else other
        lanes = pl.ds(pl.multiple_of(slot * half, half), half)
        remote(
            edge, colh.at[slot], col_ssem.at[0, 0], col_rsem.at[slot, 0], mp=other
        ).wait_recv()
        beside = colh[slot].astype(F32)
        zero = jnp.zeros_like(beside)
        left = jnp.where(col == 1, beside, zero)
        right = jnp.where(col == 0, beside, zero)
        padded[1 : rows + 1, 7:8, lanes] = left.reshape(rows, 1, half)
        padded[1 : rows + 1, 8 + cols : 9 + cols, lanes] = right.reshape(rows, 1, half)
        for way, there in ((0, above), (1, below)):
            line = 0 if way == 0 else rows + 1

            @pl.when(there)
            def _(way=way, slot=slot, lanes=lanes, line=line):
                remote(
                    patches_ref.at[0],
                    rowh.at[slot, way],
                    row_ssem.at[way, 0],
                    row_rsem.at[slot, way],
                    mp=other,
                ).wait_recv()
                remote(
                    corners.at[0],
                    cornh.at[slot, way],
                    col_ssem.at[0, 0],
                    col_rsem.at[slot, way + 1],
                    mp=other,
                ).wait_recv()
                padded[line, 8 : 8 + cols, lanes] = rowh[slot, way].astype(F32)
                packed = cornh[slot, way].astype(F32)
                corner = jnp.concatenate(
                    [packed[k : k + 1, :] for k in range(half // 128)], axis=1
                )
                blank = jnp.zeros_like(corner)
                padded[line, 7:8, lanes] = jnp.where(col == 1, corner, blank)
                padded[line, 8 + cols : 9 + cols, lanes] = jnp.where(col == 0, corner, blank)

            @pl.when(jnp.logical_not(there))
            def _(lanes=lanes, line=line):
                padded[line, :, lanes] = jnp.zeros((padded.shape[1], half), F32)

    small_copy.wait_recv()

    def stem_rows(step, carry):
        line = 2 * step
        here = pl.ds(pl.multiple_of(step * 2 * cols, 16), 2 * cols)
        parts = []
        for m in range(2):
            lanes = slice(m * half, m * half + half)
            total = padded[pl.ds(line + 1, 2), 8 : 8 + cols, lanes]
            for a in range(3):
                for b in range(3):
                    total = total + small[m, 3 * a + b : 3 * a + b + 1, :].reshape(
                        1, 1, half
                    ) * padded[pl.ds(line + a, 2), 7 + b : 7 + b + cols, lanes]
            flat = total.reshape(2 * cols, half)
            stem[m, here, :] = flat
            parts.append(flat)
        width = 2 * half
        mean_val = sum(jnp.sum(x, axis=1, keepdims=True) for x in parts) / width
        square = sum(jnp.sum(x * x, axis=1, keepdims=True) for x in parts) / width
        factor = lax.rsqrt(square - mean_val * mean_val + 1e-05)
        for m in range(2):
            nrm[here, m * half : m * half + half] = (
                (parts[m] - mean_val) * factor * small[m, 9:10, :]
            ).astype(BF16)
        return carry

    lax.fori_loop(0, rows // 2, stem_rows, 0)

    def project(c):
        return jnp.dot(nrm[...], qkvw[c], preferred_element_type=F32)

    local[1].wait()
    key = project(1)
    for p in range(pairs):
        kbuf[p] = key[:, 128 * p : 128 * p + 128].astype(BF16)
    local[2].wait()
    value = project(2)
    for p in range(pairs):
        vbuf[p] = (value[:, 128 * p : 128 * p + 128] * keep[...]).astype(BF16)

    def phi(pair):
        wide = pair.astype(F32)
        square = wide * wide
        high = square.astype(BF16)
        low = (square - high.astype(F32)).astype(BF16)
        joined = jnp.concatenate([pair, pair, high, low], axis=1)
        lifted = jnp.dot(joined, lift[...], preferred_element_type=F32)
        return (jnp.exp(lifted) * (1.0 / math.sqrt(M))).astype(BF16)

    def share(h):
        return remote(
            rs_send.at[h],
            rs_recv.at[me],
            rs_ssem.at[h],
            rs_rsem.at[me],
            tile=h // 2,
            col=lax.rem(h, 2),
        )

    def key_pair(step, carry):
        p = lax.rem(step + 1 + tile, pairs)
        feat = phi(kbuf[p])
        left = jnp.concatenate([vbuf[p], keep[...].astype(BF16)], axis=1)
        state = lax.dot_general(left, feat, (((0,), (0,)), ((), ())), preferred_element_type=F32)
        for odd in range(2):
            h = 2 * p + odd
            rs_send[h] = state[E * odd : E * odd + E, M * odd : M * odd + M].astype(BF16)
            norms[pl.ds(h, 1), :] = state[128:129, M * odd : M * odd + M]

            @pl.when(h != me)
            def _(h=h):
                share(h).start()

        return carry

    lax.fori_loop(0, pairs, key_pair, 0)
    norms_all[me] = norms[...]

    def norm_share(step):
        peer = lax.rem(me + step, group)
        return remote(
            norms_all.at[me],
            norms_all.at[me],
            nz_ssem.at[step],
            nz_rsem.at[me],
            tile=peer // 2,
            col=lax.rem(peer, 2),
        )

    for step in range(1, group):
        norm_share(step).start()
    local[3].wait()
    query = project(0)
    for p in range(pairs):
        qbuf[p] = query[:, 128 * p : 128 * p + 128].astype(BF16)

    def query_pair(p, carry):
        qfb[p] = phi(qbuf[p])
        return carry


    lax.fori_loop(0, pairs - 1, query_pair, 0)

    total = rs_send[me].astype(F32)
    for step in range(1, group):
        source = lax.rem(me + step, group)
        remote(
            rs_send.at[0], rs_recv.at[source], rs_ssem.at[0], rs_rsem.at[source], mp=other
        ).wait_recv()
        total = total + rs_recv[source].astype(F32)
    ag[me] = total.astype(BF16)

    def spread(step):
        peer = lax.rem(me + step, group)
        return remote(
            ag.at[me],
            ag.at[me],
            ag_ssem.at[step],
            ag_rsem.at[me],
            tile=peer // 2,
            col=lax.rem(peer, 2),
        )

    def arrived(h):
        remote(ag.at[h], ag.at[h], ag_ssem.at[0], ag_rsem.at[h], mp=other).wait_recv()

    for step in range(1, group):
        spread(step).start()

    query_pair(pairs - 1, 0)
    for step in range(1, group):
        source = lax.rem(me + step, group)
        remote(
            norms_all.at[0], norms_all.at[source], nz_ssem.at[0], nz_rsem.at[source], mp=other
        ).wait_recv()
    norms[...] = sum(norms_all[s] for s in range(group))

    def att_copy(p):
        return remote(
            att.at[core, p], att.at[core, p], att_ssem.at[p], att_rsem.at[core, p], mp=other
        )

    def read_pair(step, carry):
        p = lax.rem(step + tile, pairs)
        for odd in range(2):
            h = 2 * p + odd

            @pl.when(h != me)
            def _(h=h):
                arrived(h)

            rd[E * odd : E * odd + E, M * odd : M * odd + M] = ag[h]
            rd[128 + E * odd : 128 + E * odd + E, M * odd : M * odd + M] = jnp.broadcast_to(
                norms[pl.ds(h, 1), :], (E, M)
            ).astype(BF16)
        both = lax.dot_general(
            qfb[p], rd[...], (((1,), (1,)), ((), ())), preferred_element_type=F32
        )
        att[core, p] = (both[:, :128] / both[:, 128:]).astype(BF16)
        att_copy(p).start()
        return carry

    lax.fori_loop(0, pairs, read_pair, 0)

    def mix(slot):
        return jnp.dot(
            jnp.concatenate([att[slot, p] for p in range(pairs)], axis=1),
            wout[slot],
            preferred_element_type=F32,
        )

    local[4].wait()
    stem[core] = stem[core] + mix(core)
    wout_copy.wait_recv()
    for p in range(pairs):
        remote(
            att.at[core, p], att.at[other, p], att_ssem.at[p], att_rsem.at[other, p], mp=other
        ).wait_recv()
    result = stem[core] + mix(other)
    out_ref[...] = result.reshape(rows, cols, half).astype(BF16)

    for target in range(2):
        for way, there in ((0, below), (1, above)):

            @pl.when(there)
            def _(way=way, target=target):
                row_copy(way, target).wait_send()
                col_copy(way + 1, target).wait_send()

        col_copy(0, target).wait_send()
    for copy in (patch_copy, small_copy, wout_copy):
        copy.wait_send()

    def drain(h, carry):
        @pl.when(h != me)
        def _():
            share(h).wait_send()

        return carry

    lax.fori_loop(0, group, drain, 0)
    for step in range(1, group):
        spread(step).wait_send()
        norm_share(step).wait_send()
    for p in range(pairs):
        att_copy(p).wait_send()


def fused(tiles, patches, tissue, conv_weight, ln_gain, qkv_weight, omega, out_weight):
    rows, cols, half = patches.shape
    tokens = rows * cols
    group = 2 * tiles
    pairs = group // 2
    vmem, dma = pltpu.VMEM, pltpu.SemaphoreType.DMA
    anywhere = pl.BlockSpec(memory_space=pl.ANY)
    inside = pl.BlockSpec(memory_space=pltpu.VMEM)
    return pl.pallas_call(
        functools.partial(layer_kernel, tiles),
        out_shape=pltpu.VMEM(patches.shape, BF16),
        in_specs=[anywhere] * 7,
        out_specs=inside,
        scratch_shapes=[
            vmem(tissue.shape, jnp.int32),
            vmem(conv_weight.shape, BF16),
            vmem((1, half), F32),
            vmem((E, M), F32),
            vmem((2, rows, cols, half), BF16),
            vmem((rows + 2, cols + 16, 2 * half), F32),
            vmem((2, 2, cols, half), BF16),
            vmem((2, rows, half), BF16),
            vmem((rows, half), BF16),
            vmem((2, 16, 128), BF16),
            vmem((2, 2, 16, 128), BF16),
            vmem((2, 16, half), F32),
            vmem(qkv_weight.shape, BF16),
            vmem((2, half, half), BF16),
            vmem((2, tokens, half), F32),
            vmem((tokens, 2 * half), BF16),
            vmem((tokens, 128), F32),
            vmem((512, 2 * M), BF16),
            vmem((pairs, tokens, 128), BF16),
            vmem((pairs, tokens, 128), BF16),
            vmem((pairs, tokens, 128), BF16),
            vmem((pairs, tokens, 2 * M), BF16),
            vmem((group, E, M), BF16),
            vmem((group, E, M), BF16),
            vmem((group, E, M), BF16),
            vmem((group, M), F32),
            vmem((group, group, M), F32),
            vmem((256, 2 * M), BF16),
            vmem((2, pairs, tokens, 128), BF16),
            dma((9,)),
            dma((2,)),
            dma((2, 2)),
            dma((2, 2)),
            dma((3, 2)),
            dma((2, 3)),
            dma((2,)),
            dma((2,)),
            dma((group,)),
            dma((group,)),
            dma((group,)),
            dma((group,)),
            dma((pairs,)),
            dma((2, pairs)),
            dma((group,)),
            dma((group,)),
        ],
        compiler_params=pltpu.CompilerParams(
            collective_id=0, has_side_effects=True, vmem_limit_bytes=63 * 2**20
        ),
    )(patches, tissue, conv_weight, ln_gain.reshape(1, half), qkv_weight, omega.T, out_weight)


def solution(mesh):
    tiles, sides, cores = mesh.shape["tile"], mesh.shape["col"], mesh.shape["mp"]

    def body(*args):
        heads_here = args[4].shape[2] // E
        if sides == 2 and cores == 2 and tiles * sides == heads_here:
            return fused(tiles, *args)
        return shards(*args)

    placed = (
        P(("slides", "tile"), "col", "mp"),
        P(("slides", "tile"), "col"),
        P(None, None, "mp"),
        P("mp"),
        P(None, None, "mp"),
        P(),
        P("mp", None),
    )
    return jax.shard_map(
        body,
        mesh=mesh,
        in_specs=placed,
        out_specs=P(("slides", "tile"), "col", "mp"),
        check_vma=False,
    )
```
